32 devices in a mesh: ctx: 8 (over y, x, core), fsdp: 4 (over z).
Axes of the slice: x: 2, y: 2, z: 4, core: 2. Of those that a mesh axis runs over, the one named last changes fastest.
Arguments:
- layer_in: bfloat16 [4, 8, 192, 768], P('fsdp', 'ctx'), may hold values from -6 to 6
- qkv_weight: bfloat16 [768, 2304], P('fsdp'), may hold values from -0.21875 to 0.21875
- query_bias: float32 [768], replicated, may hold values from -3 to 3
- value_bias: float32 [768], replicated, may hold values from -3 to 3
- out_weight: bfloat16 [768, 768], P('fsdp'), may hold values from -1.5 to 1.5
- out_bias: float32 [768], replicated, may hold values from -3 to 3
- fc_weight: bfloat16 [768, 3072], P('fsdp'), may hold values from -0.21875 to 0.21875
- fc_bias: float32 [3072], replicated, may hold values from -3 to 3
- proj_weight: bfloat16 [3072, 768], P('fsdp'), may hold values from -0.109375 to 0.109375
- proj_bias: float32 [768], replicated, may hold values from -3 to 3
- attn_norm_gain: float32 [768], replicated, may hold values from 0.5 to 1.5
- attn_norm_shift: float32 [768], replicated, may hold values from -2 to 2
- mlp_norm_gain: float32 [768], replicated, may hold values from 0.5 to 1.5
- mlp_norm_shift: float32 [768], replicated, may hold values from -2 to 2
- cotangent: bfloat16 [4, 8, 192, 768], P('fsdp', 'ctx'), may hold values from -6 to 6
- pair_table: int32 [8], replicated, may hold values from 0 to 7, each once
Outputs:
- layer_out: bfloat16 [4, 8, 192, 768], P('fsdp', 'ctx')
- grad_in: float32 [4, 8, 192, 768], P('fsdp', 'ctx')
- grad_qkv_weight: float32 [768, 2304], P(('ctx', 'fsdp'))
- grad_query_bias: float32 [768], P(('ctx', 'fsdp'))
- grad_value_bias: float32 [768], P(('ctx', 'fsdp'))
- grad_out_weight: float32 [768, 768], P(('ctx', 'fsdp'))
- grad_out_bias: float32 [768], P(('ctx', 'fsdp'))
- grad_fc_weight: float32 [768, 3072], P(('ctx', 'fsdp'))
- grad_fc_bias: float32 [3072], P(('ctx', 'fsdp'))
- grad_proj_weight: float32 [3072, 768], P(('ctx', 'fsdp'))
- grad_proj_bias: float32 [768], P(('ctx', 'fsdp'))
- grad_attn_norm_gain: float32 [768], P(('ctx', 'fsdp'))
- grad_attn_norm_shift: float32 [768], P(('ctx', 'fsdp'))
- grad_mlp_norm_gain: float32 [768], P(('ctx', 'fsdp'))
- grad_mlp_norm_shift: float32 [768], P(('ctx', 'fsdp'))
The draws below stay inside these ranges and needn't reach their ends.
Inputs may be any that keep to these rules, and one draw needn't show every extreme that they name: pair_table is a permutation: index c of ctx holds blocks pair_table[c] and 15 - pair_table[c] of every sequence.
All inputs are finite; a program needn't handle non-finite values.
Results may differ from the reference program's by a relative error of at most 0.035.
Values may be sent and summed in bfloat16 or wider, within the bound.
A program may use at most 256 MiB of HBM per device.

```python
import jax
import jax.numpy as jnp
from jax import lax

D = 768
H = 12
HEAD_DIM = 64
FF = 3072
BLK = 96
SEQ_ALL = 4
N_CTX = 8


def levels(key, dims, cuts, low, high):
    factor_of, own = 1.0, jax.random.fold_in(key, 6)
    for dim, parts in cuts:
        draws = jnp.exp(jax.random.uniform(jax.random.fold_in(own, dim), (parts,), jnp.float32, low / len(cuts), high / len(cuts)))
        factor_of = factor_of * jnp.repeat(draws, dims[dim] // parts).reshape([-1 if axis == dim else 1 for axis in range(len(dims))])
    return factor_of


def normal_values(own_key, dims, scale, most, shards=(), kind=jnp.bfloat16):
    drawn = scale * jax.random.normal(own_key, dims, jnp.float32)
    if shards:
        drawn = drawn * levels(own_key, dims, shards, -0.22, 0.18)
    return jnp.clip(drawn, -most, most).astype(kind)


def setup_inputs(seed: int = 0) -> dict:
    seeds = jax.random.split(jax.random.key(seed), 17)
    layer_in = normal_values(seeds[0], (SEQ_ALL, N_CTX, 2 * BLK, D), 1.0, 6.0, ((0, 4), (1, 8)))
    qkv_weight = normal_values(seeds[1], (D, 3 * D), D ** -0.5, 0.21875, ((0, 4),))
    query_bias = normal_values(seeds[2], (D,), 0.5, 3.0, (), jnp.float32)
    value_bias = normal_values(seeds[3], (D,), 0.5, 3.0, (), jnp.float32)
    out_weight = normal_values(seeds[4], (D, D), 16 ** -0.5, 1.5, ((0, 4),))
    out_bias = normal_values(seeds[5], (D,), 0.5, 3.0, (), jnp.float32)
    fc_weight = normal_values(seeds[6], (D, FF), D ** -0.5, 0.21875, ((0, 4),))
    fc_bias = normal_values(seeds[7], (FF,), 0.5, 3.0, (), jnp.float32)
    proj_weight = normal_values(seeds[8], (FF, D), FF ** -0.5, 0.109375, ((0, 4),))
    proj_bias = normal_values(seeds[9], (D,), 0.5, 3.0, (), jnp.float32)
    attn_norm_gain = jnp.clip(1.0 + 0.1 * jax.random.normal(seeds[10], (D,), jnp.float32), 0.5, 1.5)
    attn_norm_shift = normal_values(seeds[11], (D,), 0.3, 2.0, (), jnp.float32)
    mlp_norm_gain = jnp.clip(1.0 + 0.1 * jax.random.normal(seeds[12], (D,), jnp.float32), 0.5, 1.5)
    mlp_norm_shift = normal_values(seeds[13], (D,), 0.3, 2.0, (), jnp.float32)
    cotangent = normal_values(seeds[14], (SEQ_ALL, N_CTX, 2 * BLK, D), 1.0, 6.0, ((0, 4), (1, 8)))
    pair_table = jax.random.permutation(seeds[15], N_CTX).astype(jnp.int32)
    return dict(layer_in=layer_in, qkv_weight=qkv_weight, query_bias=query_bias, value_bias=value_bias, out_weight=out_weight, out_bias=out_bias, fc_weight=fc_weight, fc_bias=fc_bias, proj_weight=proj_weight, proj_bias=proj_bias, attn_norm_gain=attn_norm_gain, attn_norm_shift=attn_norm_shift, mlp_norm_gain=mlp_norm_gain, mlp_norm_shift=mlp_norm_shift, cotangent=cotangent, pair_table=pair_table)


@jax.custom_vjp
def low(v):
    return lax.optimization_barrier(v.astype(jnp.bfloat16)).astype(jnp.float32)

@jax.custom_vjp
def low_back(v):
    return v

def low_keep(v):
    return (low(v), None)

def low_pass(kept, grad):
    return (grad,)

def back_keep(v):
    return (v, None)

def back_low(kept, grad):
    return (low(grad),)
low.defvjp(low_keep, low_pass)
low_back.defvjp(back_keep, back_low)
epsilon = 1e-05
masked_score = -1e+30
highest = lax.Precision.HIGHEST

def layer_norm(values, gain, shift):
    centered = values - lax.optimization_barrier(jnp.mean(values, axis=-1, keepdims=True))
    variance = lax.optimization_barrier(jnp.mean(centered * centered, axis=-1, keepdims=True))
    return centered * lax.rsqrt(variance + epsilon) * gain + shift

def matmul(left, right):
    return jnp.dot(left, right, precision=highest)

def positions(pair_table):
    column = jnp.arange(2 * BLK, dtype=jnp.int32)[None, :]
    pair_index = pair_table.astype(jnp.int32)[:, None]
    lower = pair_index * BLK + column
    upper = (2 * N_CTX - 1 - pair_index) * BLK + column - BLK
    return jnp.where(column < BLK, lower, upper)

def attend(query, keys, values, key_pos):
    length = query.shape[0]
    block = 512 if length % 512 == 0 else length
    query_heads = query.reshape(length // block, block, H, HEAD_DIM)
    pos_blocks = key_pos.reshape(length // block, block)
    key_heads = keys.reshape(length, H, HEAD_DIM)
    value_heads = values.reshape(length, H, HEAD_DIM)

    def one_block(pieces):
        query_blk, query_pos = pieces
        scores = jnp.einsum('qhe,khe->hqk', query_blk, key_heads, precision=highest) * HEAD_DIM ** (-0.5)
        scores = low_back(scores)
        allowed = key_pos[None, None, :] <= query_pos[None, :, None]
        weights = low(jax.nn.softmax(jnp.where(allowed, scores, masked_score), axis=-1))
        return jnp.einsum('hqk,khe->qhe', weights, value_heads, precision=highest)
    mixed = lax.map(jax.checkpoint(one_block), (query_heads, pos_blocks))
    return mixed.reshape(length, H * HEAD_DIM)

def forward(seq_in, qkv_weight, query_bias, value_bias, out_weight, out_bias, fc_weight, fc_bias, proj_weight, proj_bias, attn_norm_gain, attn_norm_shift, mlp_norm_gain, mlp_norm_shift, key_pos):
    first_in = low(layer_norm(seq_in, attn_norm_gain, attn_norm_shift))
    projected = matmul(first_in, qkv_weight)
    query = low(low_back(projected[:, :D] + query_bias))
    keys = low(low_back(projected[:, D:2 * D]))
    values = low(low_back(projected[:, 2 * D:] + value_bias))
    attended = low(low_back(attend(query, keys, values, key_pos)))
    middle = seq_in + low_back(matmul(attended, out_weight)) + out_bias
    second_in = low(layer_norm(middle, mlp_norm_gain, mlp_norm_shift))
    pre_act = low_back(matmul(second_in, fc_weight) + fc_bias)
    activated = low(jax.nn.gelu(pre_act, approximate=True))
    return middle + matmul(activated, proj_weight) + proj_bias

def reference(layer_in, qkv_weight, query_bias, value_bias, out_weight, out_bias, fc_weight, fc_bias, proj_weight, proj_bias, attn_norm_gain, attn_norm_shift, mlp_norm_gain, mlp_norm_shift, cotangent, pair_table):
    key_pos = positions(pair_table).reshape(-1)
    params = tuple((item.astype(jnp.float32) for item in (qkv_weight, query_bias, value_bias, out_weight, out_bias, fc_weight, fc_bias, proj_weight, proj_bias, attn_norm_gain, attn_norm_shift, mlp_norm_gain, mlp_norm_shift)))
    seq_count = layer_in.shape[0]
    flat_in = layer_in.reshape(seq_count, -1, D).astype(jnp.float32)
    flat_cot = cotangent.reshape(seq_count, -1, D).astype(jnp.float32)

    def whole(inputs, weights):
        return forward(inputs, *weights, key_pos)

    def one_sequence(totals, pieces):
        seq_in, seq_cot = pieces
        output, pullback = jax.vjp(whole, seq_in, params)
        grad_seq, grad_params = pullback(seq_cot)
        totals = jax.tree.map(jnp.add, totals, grad_params)
        return (totals, (output, grad_seq))
    zeros = jax.tree.map(jnp.zeros_like, params)
    totals, (outputs, grads_seq) = lax.scan(one_sequence, zeros, (flat_in, flat_cot))
    layer_out = outputs.astype(jnp.bfloat16).reshape(layer_in.shape)
    grad_in = grads_seq.reshape(layer_in.shape)
    return (layer_out, grad_in, totals[0], totals[1], totals[2], totals[3], totals[4], totals[5], totals[6], totals[7], totals[8], totals[9], totals[10], totals[11], totals[12])
```

```python
from functools import partial

import jax
import jax.numpy as jnp
from jax import lax
from jax.experimental import pallas as pl
from jax.experimental.pallas import tpu as pltpu
from jax.sharding import PartitionSpec as P

H = 12
HEAD_DIM = 64
BLK = 96


epsilon = 1e-05
masked_score = -1e30


def normalize(values):
    centered = values - jnp.mean(values, axis=-1, keepdims=True)
    inverse = lax.rsqrt(jnp.mean(centered * centered, axis=-1, keepdims=True) + epsilon)
    return (centered * inverse, inverse)


def norm_back(grad_out, normed, inverse, gain):
    scaled = grad_out * gain
    grad_input = inverse * (
        scaled
        - jnp.mean(scaled, axis=-1, keepdims=True)
        - normed * jnp.mean(scaled * normed, axis=-1, keepdims=True)
    )
    return (grad_input, jnp.sum(grad_out * normed, axis=0), jnp.sum(grad_out, axis=0))


def block_positions(pair_table, device, ctx_count):
    pair_index = lax.dynamic_index_in_dim(pair_table, device, 0, keepdims=False)
    column = jnp.arange(2 * BLK, dtype=jnp.int32)
    lower = pair_index * BLK + column
    upper = (2 * ctx_count - 1 - pair_index) * BLK + column - BLK
    return jnp.where(column < BLK, lower, upper)


PAIR = 2 * HEAD_DIM
CHUNK = 8 * 2 * BLK
NT = (((1,), (1,)), ((), ()))


def chunk_of(total):
    return CHUNK if total % CHUNK == 0 else total


def head_only(block, head):
    lane = lax.broadcasted_iota(jnp.int32, block.shape, 1)
    return jnp.where((lane // HEAD_DIM) == head, block, jnp.zeros_like(block))


def head_pick(first, second):
    lane = lax.broadcasted_iota(jnp.int32, first.shape, 1)
    return jnp.where(lane < HEAD_DIM, first, second)


def dot_nt(left, right):
    return lax.dot_general(left, right, NT, preferred_element_type=jnp.float32)


def dot_nn(left, right):
    return jnp.dot(left, right, preferred_element_type=jnp.float32)


def forward_kernel(qpos_ref, kpos_ref, q_ref, k_ref, v_ref, out_ref, lse_ref, max_ref, sum_ref):
    step = pl.program_id(1)
    last = pl.num_programs(1) - 1

    @pl.when(step == 0)
    def _():
        max_ref[...] = jnp.full_like(max_ref, masked_score)
        sum_ref[...] = jnp.zeros_like(sum_ref)
        out_ref[...] = jnp.zeros_like(out_ref)

    allowed = kpos_ref[...] <= qpos_ref[...]
    query, keys, values = q_ref[...], k_ref[...], v_ref[...]
    mixed, factors = [], []
    for head in range(2):
        scores = jnp.where(allowed, dot_nt(head_only(query, head), keys), masked_score)
        old_max = max_ref[head]
        new_max = jnp.maximum(old_max, jnp.max(scores, axis=-1, keepdims=True))
        expd = jnp.exp(scores - new_max)
        factor = jnp.exp(old_max - new_max)
        sum_ref[head] = sum_ref[head] * factor + jnp.sum(expd, axis=-1, keepdims=True)
        max_ref[head] = new_max
        mixed.append(dot_nn(expd.astype(jnp.bfloat16), values))
        factors.append(factor)
    rows = query.shape[0]
    scale = head_pick(*(jnp.broadcast_to(f, (rows, PAIR)) for f in factors))
    out_ref[...] = out_ref[...] * scale + head_pick(mixed[0], mixed[1])

    @pl.when(step == last)
    def _():
        total = head_pick(*(jnp.broadcast_to(sum_ref[h], (rows, PAIR)) for h in range(2)))
        out_ref[...] = out_ref[...] / total
        lse_ref[0] = jnp.concatenate(
            [max_ref[h] + jnp.log(sum_ref[h]) for h in range(2)], axis=-1
        )


def forward_attention(query_pos, key_pos, query, keys_values):
    rows, width = query.shape
    total = keys_values.shape[0]
    chunk = chunk_of(total)
    pairs = width // PAIR
    return pl.pallas_call(
        forward_kernel,
        grid=(pairs, total // chunk),
        in_specs=[
            pl.BlockSpec((rows, 1), lambda h, c: (0, 0)),
            pl.BlockSpec((1, chunk), lambda h, c: (0, c)),
            pl.BlockSpec((rows, PAIR), lambda h, c: (0, h)),
            pl.BlockSpec((chunk, PAIR), lambda h, c: (c, h)),
            pl.BlockSpec((chunk, PAIR), lambda h, c: (c, h + pairs)),
        ],
        out_specs=[
            pl.BlockSpec((rows, PAIR), lambda h, c: (0, h)),
            pl.BlockSpec((1, rows, 2), lambda h, c: (h, 0, 0)),
        ],
        out_shape=[
            jax.ShapeDtypeStruct((rows, width), jnp.float32),
            jax.ShapeDtypeStruct((pairs, rows, 2), jnp.float32),
        ],
        scratch_shapes=[
            pltpu.VMEM((2, rows, 1), jnp.float32),
            pltpu.VMEM((2, rows, 1), jnp.float32),
        ],
        compiler_params=pltpu.CompilerParams(vmem_limit_bytes=40 * 2**20),
        cost_estimate=pl.CostEstimate(
            flops=8 * rows * total * width,
            bytes_accessed=4 * total * width,
            transcendentals=rows * total * H,
        ),
        name="attention_forward",
    )(query_pos[:, None], key_pos[None, :], query, keys_values, keys_values)


def query_kernel(qpos_ref, kpos_ref, q_ref, do_ref, stat_ref, k_ref, v_ref, dq_ref):
    @pl.when(pl.program_id(1) == 0)
    def _():
        dq_ref[...] = jnp.zeros_like(dq_ref)

    allowed = kpos_ref[...] <= qpos_ref[...]
    query, d_out, keys, values = q_ref[...], do_ref[...], k_ref[...], v_ref[...]
    parts = []
    for head in range(2):
        lse = stat_ref[0, :, head : head + 1]
        delta = stat_ref[0, :, head + 2 : head + 3]
        scores = jnp.where(allowed, dot_nt(head_only(query, head), keys), masked_score)
        prob = jnp.exp(scores - lse)
        d_prob = dot_nt(head_only(d_out, head), values)
        d_score = (prob * (d_prob - delta)).astype(jnp.bfloat16)
        parts.append(dot_nn(d_score, keys))
    dq_ref[...] += head_pick(parts[0], parts[1]) * HEAD_DIM ** (-0.5)


def query_gradient(query_pos, key_pos, query, d_out, stats, keys_values):
    rows, width = query.shape
    total = keys_values.shape[0]
    chunk = chunk_of(total)
    pairs = width // PAIR
    return pl.pallas_call(
        query_kernel,
        grid=(pairs, total // chunk),
        in_specs=[
            pl.BlockSpec((rows, 1), lambda h, c: (0, 0)),
            pl.BlockSpec((1, chunk), lambda h, c: (0, c)),
            pl.BlockSpec((rows, PAIR), lambda h, c: (0, h)),
            pl.BlockSpec((rows, PAIR), lambda h, c: (0, h)),
            pl.BlockSpec((1, rows, 4), lambda h, c: (h, 0, 0)),
            pl.BlockSpec((chunk, PAIR), lambda h, c: (c, h)),
            pl.BlockSpec((chunk, PAIR), lambda h, c: (c, h + pairs)),
        ],
        out_specs=pl.BlockSpec((rows, PAIR), lambda h, c: (0, h)),
        out_shape=jax.ShapeDtypeStruct((rows, width), jnp.float32),
        compiler_params=pltpu.CompilerParams(vmem_limit_bytes=40 * 2**20),
        cost_estimate=pl.CostEstimate(
            flops=12 * rows * total * width,
            bytes_accessed=4 * total * width,
            transcendentals=rows * total * H,
        ),
        name="attention_query_gradient",
    )(query_pos[:, None], key_pos[None, :], query, d_out, stats, keys_values, keys_values)


def key_kernel(kpos_ref, qpos_ref, k_ref, v_ref, q_ref, do_ref, stat_ref, dk_ref, dv_ref):
    @pl.when(pl.program_id(1) == 0)
    def _():
        dk_ref[...] = jnp.zeros_like(dk_ref)
        dv_ref[...] = jnp.zeros_like(dv_ref)

    allowed = kpos_ref[...] <= qpos_ref[...]
    keys, values, query, d_out = k_ref[...], v_ref[...], q_ref[...], do_ref[...]
    key_parts, value_parts = [], []
    for head in range(2):
        lse = stat_ref[0, head : head + 1, :]
        delta = stat_ref[0, head + 2 : head + 3, :]
        scores = jnp.where(allowed, dot_nt(head_only(keys, head), query), masked_score)
        prob = jnp.exp(scores - lse)
        value_parts.append(dot_nn(prob.astype(jnp.bfloat16), d_out))
        d_prob = dot_nt(head_only(values, head), d_out)
        d_score = (prob * (d_prob - delta)).astype(jnp.bfloat16)
        key_parts.append(dot_nn(d_score, query))
    dk_ref[...] += head_pick(key_parts[0], key_parts[1])
    dv_ref[...] += head_pick(value_parts[0], value_parts[1])


def key_gradients(key_pos, query_pos, qkv, query_all, d_out_all, stats_all):
    rows = qkv.shape[0]
    total, width = query_all.shape
    chunk = chunk_of(total)
    pairs = width // PAIR
    grad_spec = pl.BlockSpec((rows, PAIR), lambda h, c: (0, h))
    return pl.pallas_call(
        key_kernel,
        grid=(pairs, total // chunk),
        in_specs=[
            pl.BlockSpec((rows, 1), lambda h, c: (0, 0)),
            pl.BlockSpec((1, chunk), lambda h, c: (0, c)),
            pl.BlockSpec((rows, PAIR), lambda h, c: (0, h)),
            pl.BlockSpec((rows, PAIR), lambda h, c: (0, h + pairs)),
            pl.BlockSpec((chunk, PAIR), lambda h, c: (c, h)),
            pl.BlockSpec((chunk, PAIR), lambda h, c: (c, h)),
            pl.BlockSpec((1, 4, chunk), lambda h, c: (h, 0, c)),
        ],
        out_specs=[grad_spec, grad_spec],
        out_shape=[jax.ShapeDtypeStruct((rows, width), jnp.float32)] * 2,
        compiler_params=pltpu.CompilerParams(vmem_limit_bytes=40 * 2**20),
        cost_estimate=pl.CostEstimate(
            flops=16 * rows * total * width,
            bytes_accessed=4 * total * width,
            transcendentals=rows * total * H,
        ),
        name="attention_key_gradients",
    )(key_pos[:, None], query_pos[None, :], qkv, qkv, query_all, d_out_all, stats_all)


def whole_weight(weight):
    share = weight.shape[0] // lax.axis_size("ctx")
    mine = lax.dynamic_slice_in_dim(weight, lax.axis_index("ctx") * share, share, 0)
    return lax.all_gather(mine, ("fsdp", "ctx"), axis=0, tiled=True)


def all_positions(pair_table, ctx_count):
    column = jnp.arange(2 * BLK, dtype=jnp.int32)[None, :]
    pair = pair_table[:, None]
    lower = pair * BLK + column
    upper = (2 * ctx_count - 1 - pair) * BLK + column - BLK
    return jnp.where(column < BLK, lower, upper).reshape(-1)


def scatter(term):
    return lax.psum_scatter(term, ("ctx", "fsdp"), scatter_dimension=0, tiled=True)


def per_device(
    layer_in,
    qkv_weight,
    query_bias,
    value_bias,
    out_weight,
    out_bias,
    fc_weight,
    fc_bias,
    proj_weight,
    proj_bias,
    attn_norm_gain,
    attn_norm_shift,
    mlp_norm_gain,
    mlp_norm_shift,
    cotangent,
    pair_table,
):
    ctx_count = lax.axis_size("ctx")
    shards = ctx_count * lax.axis_size("fsdp")
    _, _, rows, width = layer_in.shape
    my_pos = block_positions(pair_table, lax.axis_index("ctx"), ctx_count)
    every_pos = all_positions(pair_table, ctx_count)
    flat_in = layer_in.reshape(rows, width).astype(jnp.float32)
    full_qkv = whole_weight(qkv_weight)
    full_out = whole_weight(out_weight)
    full_fc = whole_weight(fc_weight)
    full_proj = whole_weight(proj_weight)
    normed_one, inverse_one = normalize(flat_in)
    first_in = (normed_one * attn_norm_gain + attn_norm_shift).astype(jnp.bfloat16)
    keys_values = (
        jnp.dot(first_in, full_qkv[:, width:], preferred_element_type=jnp.float32)
        + jnp.concatenate([jnp.zeros_like(value_bias), value_bias])
    ).astype(jnp.bfloat16)
    every_kv = lax.all_gather(keys_values, "ctx", axis=0, tiled=True)
    query = (
        jnp.dot(first_in, full_qkv[:, :width], preferred_element_type=jnp.float32) + query_bias
    ).astype(jnp.bfloat16) * jnp.bfloat16(HEAD_DIM ** (-0.5))
    every_query = lax.all_gather(query, "ctx", axis=0, tiled=True)
    attn_exact, lse = forward_attention(my_pos, every_pos, query, every_kv)
    attended = attn_exact.astype(jnp.bfloat16)
    middle = flat_in + jnp.dot(attended, full_out, preferred_element_type=jnp.float32) + out_bias
    normed_two, inverse_two = normalize(middle)
    second_in = (normed_two * mlp_norm_gain + mlp_norm_shift).astype(jnp.bfloat16)
    pre_act = jnp.dot(second_in, full_fc, preferred_element_type=jnp.float32) + fc_bias
    activated, gelu_back = jax.vjp(partial(jax.nn.gelu, approximate=True), pre_act)
    act_low = activated.astype(jnp.bfloat16)
    result = middle + jnp.dot(act_low, full_proj, preferred_element_type=jnp.float32) + proj_bias
    layer_out = result.astype(jnp.bfloat16).reshape(layer_in.shape)
    d_result = cotangent.reshape(rows, width)
    d_act = jnp.einsum("td,fd->tf", d_result, full_proj, preferred_element_type=jnp.float32)
    (d_pre,) = gelu_back(d_act)
    d_pre_low = d_pre.astype(jnp.bfloat16)
    d_second = jnp.einsum("tf,df->td", d_pre_low, full_fc, preferred_element_type=jnp.float32)
    d_mid_norm, grad_mlp_gain, grad_mlp_shift = norm_back(
        d_second, normed_two, inverse_two, mlp_norm_gain
    )
    d_middle = d_result.astype(jnp.float32) + d_mid_norm
    d_branch = d_middle.astype(jnp.bfloat16)
    d_attended = jnp.einsum(
        "te,de->td", d_branch, full_out, preferred_element_type=jnp.float32
    ).astype(jnp.bfloat16)
    delta = jnp.sum(
        (d_attended.astype(jnp.float32) * attn_exact).reshape(rows, width // PAIR, 2, HEAD_DIM),
        axis=-1,
    )
    stats = jnp.concatenate([lse, jnp.transpose(delta, (1, 0, 2))], axis=-1)
    every_d_out = lax.all_gather(d_attended, "ctx", axis=0, tiled=True)
    every_stat = lax.all_gather(
        jnp.transpose(stats, (0, 2, 1)).reshape(-1, rows), "ctx", axis=1, tiled=True
    ).reshape(width // PAIR, 4, ctx_count * rows)
    grad_proj = jnp.einsum("tf,td->fd", act_low, d_result, preferred_element_type=jnp.float32)
    grad_fc = jnp.einsum("td,tf->df", second_in, d_pre_low, preferred_element_type=jnp.float32)
    grad_out = jnp.einsum("td,te->de", attended, d_branch, preferred_element_type=jnp.float32)
    sum_proj = scatter(grad_proj.astype(jnp.bfloat16))
    sum_fc = scatter(grad_fc.astype(jnp.bfloat16))
    sum_out = scatter(grad_out.astype(jnp.bfloat16))
    d_query = query_gradient(my_pos, every_pos, query, d_attended, stats, every_kv)
    d_key, d_value = key_gradients(
        my_pos, every_pos, keys_values, every_query, every_d_out, every_stat
    )
    d_qkv = jnp.concatenate([d_query, d_key, d_value], axis=1).astype(jnp.bfloat16)
    grad_qkv = jnp.einsum("td,te->de", first_in, d_qkv, preferred_element_type=jnp.float32)
    d_first = jnp.einsum("te,de->td", d_qkv, full_qkv, preferred_element_type=jnp.float32)
    d_in_norm, grad_attn_gain, grad_attn_shift = norm_back(
        d_first, normed_one, inverse_one, attn_norm_gain
    )
    grad_in = (d_middle + d_in_norm).reshape(layer_in.shape)
    bias_sum = jnp.sum(d_qkv.astype(jnp.float32), axis=0)
    vectors = (
        bias_sum[:width],
        bias_sum[2 * width :],
        jnp.sum(d_middle, axis=0),
        jnp.sum(d_pre_low.astype(jnp.float32), axis=0),
        jnp.sum(d_result.astype(jnp.float32), axis=0),
        grad_attn_gain,
        grad_attn_shift,
        grad_mlp_gain,
        grad_mlp_shift,
    )
    packed = jnp.concatenate([item.reshape(shards, -1) for item in vectors], axis=1)
    spare = -packed.shape[1] % 128
    packed = jnp.pad(packed, ((0, 0), (0, spare)))
    grad_qkv_low, packed, sum_proj, sum_fc, sum_out = lax.optimization_barrier(
        (grad_qkv.astype(jnp.bfloat16), packed, sum_proj, sum_fc, sum_out)
    )
    sum_qkv = scatter(grad_qkv_low).astype(jnp.float32)
    sum_small = scatter(packed)[0]
    small, start = [], 0
    for item in vectors:
        size = item.shape[0] // shards
        small.append(sum_small[start : start + size])
        start += size
    return (
        layer_out,
        grad_in,
        sum_qkv,
        small[0],
        small[1],
        sum_out.astype(jnp.float32),
        small[2],
        sum_fc.astype(jnp.float32),
        small[3],
        sum_proj.astype(jnp.float32),
        small[4],
        small[5],
        small[6],
        small[7],
        small[8],
    )


def solution(mesh):
    return jax.shard_map(
        per_device,
        mesh=mesh,
        in_specs=(
            P("fsdp", "ctx", None, None),
            P("fsdp", None),
            P(),
            P(),
            P("fsdp", None),
            P(),
            P("fsdp", None),
            P(),
            P("fsdp", None),
            P(),
            P(),
            P(),
            P(),
            P(),
            P("fsdp", "ctx", None, None),
            P(),
        ),
        out_specs=(
            P("fsdp", "ctx", None, None),
            P("fsdp", "ctx", None, None),
            P(("ctx", "fsdp"), None),
            P(("ctx", "fsdp")),
            P(("ctx", "fsdp")),
            P(("ctx", "fsdp"), None),
            P(("ctx", "fsdp")),
            P(("ctx", "fsdp"), None),
            P(("ctx", "fsdp")),
            P(("ctx", "fsdp"), None),
            P(("ctx", "fsdp")),
            P(("ctx", "fsdp")),
            P(("ctx", "fsdp")),
            P(("ctx", "fsdp")),
            P(("ctx", "fsdp")),
        ),
        check_vma=False,
    )
```

```python
from functools import partial

import jax
import jax.numpy as jnp
from jax import lax
from jax.experimental import pallas as pl
from jax.experimental.pallas import tpu as pltpu
from jax.sharding import PartitionSpec as P

H = 12
HEAD_DIM = 64
BLK = 96


epsilon = 1e-05
masked_score = -1e30


def normalize(values):
    centered = values - jnp.mean(values, axis=-1, keepdims=True)
    inverse = lax.rsqrt(jnp.mean(centered * centered, axis=-1, keepdims=True) + epsilon)
    return (centered * inverse, inverse)


def norm_back(grad_out, normed, inverse, gain):
    scaled = grad_out * gain
    grad_input = inverse * (
        scaled
        - jnp.mean(scaled, axis=-1, keepdims=True)
        - normed * jnp.mean(scaled * normed, axis=-1, keepdims=True)
    )
    return (grad_input, jnp.sum(grad_out * normed, axis=0), jnp.sum(grad_out, axis=0))


def block_positions(pair_table, device, ctx_count):
    pair_index = lax.dynamic_index_in_dim(pair_table, device, 0, keepdims=False)
    column = jnp.arange(2 * BLK, dtype=jnp.int32)
    lower = pair_index * BLK + column
    upper = (2 * ctx_count - 1 - pair_index) * BLK + column - BLK
    return jnp.where(column < BLK, lower, upper)


PAIR = 2 * HEAD_DIM
CHUNK = 8 * 2 * BLK
NT = (((1,), (1,)), ((), ()))


def chunk_of(total):
    return CHUNK if total % CHUNK == 0 else total


def head_only(block, head):
    lane = lax.broadcasted_iota(jnp.int32, block.shape, 1)
    return jnp.where((lane // HEAD_DIM) == head, block, jnp.zeros_like(block))


def head_pick(first, second):
    lane = lax.broadcasted_iota(jnp.int32, first.shape, 1)
    return jnp.where(lane < HEAD_DIM, first, second)


def dot_nt(left, right):
    return lax.dot_general(left, right, NT, preferred_element_type=jnp.float32)


def dot_nn(left, right):
    return jnp.dot(left, right, preferred_element_type=jnp.float32)


def forward_kernel(qpos_ref, kpos_ref, q_ref, k_ref, v_ref, out_ref, lse_ref, max_ref, sum_ref):
    step = pl.program_id(1)
    last = pl.num_programs(1) - 1

    @pl.when(step == 0)
    def _():
        max_ref[...] = jnp.full_like(max_ref, masked_score)
        sum_ref[...] = jnp.zeros_like(sum_ref)
        out_ref[...] = jnp.zeros_like(out_ref)

    allowed = kpos_ref[...] <= qpos_ref[...]
    query, keys, values = q_ref[...], k_ref[...], v_ref[...]
    mixed, factors = [], []
    for head in range(2):
        scores = jnp.where(allowed, dot_nt(head_only(query, head), keys), masked_score)
        old_max = max_ref[head]
        new_max = jnp.maximum(old_max, jnp.max(scores, axis=-1, keepdims=True))
        expd = jnp.exp(scores - new_max)
        factor = jnp.exp(old_max - new_max)
        sum_ref[head] = sum_ref[head] * factor + jnp.sum(expd, axis=-1, keepdims=True)
        max_ref[head] = new_max
        mixed.append(dot_nn(expd.astype(jnp.bfloat16), values))
        factors.append(factor)
    rows = query.shape[0]
    scale = head_pick(*(jnp.broadcast_to(f, (rows, PAIR)) for f in factors))
    out_ref[...] = out_ref[...] * scale + head_pick(mixed[0], mixed[1])

    @pl.when(step == last)
    def _():
        total = head_pick(*(jnp.broadcast_to(sum_ref[h], (rows, PAIR)) for h in range(2)))
        out_ref[...] = out_ref[...] / total
        lse_ref[0] = jnp.concatenate(
            [max_ref[h] + jnp.log(sum_ref[h]) for h in range(2)], axis=-1
        )


def forward_attention(query_pos, key_pos, query, keys_values):
    rows, width = query.shape
    total = keys_values.shape[0]
    chunk = chunk_of(total)
    pairs = width // PAIR
    return pl.pallas_call(
        forward_kernel,
        grid=(pairs, total // chunk),
        in_specs=[
            pl.BlockSpec((rows, 1), lambda h, c: (0, 0)),
            pl.BlockSpec((1, chunk), lambda h, c: (0, c)),
            pl.BlockSpec((rows, PAIR), lambda h, c: (0, h)),
            pl.BlockSpec((chunk, PAIR), lambda h, c: (c, h)),
            pl.BlockSpec((chunk, PAIR), lambda h, c: (c, h + pairs)),
        ],
        out_specs=[
            pl.BlockSpec((rows, PAIR), lambda h, c: (0, h)),
            pl.BlockSpec((1, rows, 2), lambda h, c: (h, 0, 0)),
        ],
        out_shape=[
            jax.ShapeDtypeStruct((rows, width), jnp.float32),
            jax.ShapeDtypeStruct((pairs, rows, 2), jnp.float32),
        ],
        scratch_shapes=[
            pltpu.VMEM((2, rows, 1), jnp.float32),
            pltpu.VMEM((2, rows, 1), jnp.float32),
        ],
        compiler_params=pltpu.CompilerParams(vmem_limit_bytes=40 * 2**20),
        cost_estimate=pl.CostEstimate(
            flops=8 * rows * total * width,
            bytes_accessed=4 * total * width,
            transcendentals=rows * total * H,
        ),
        name="attention_forward",
    )(query_pos[:, None], key_pos[None, :], query, keys_values, keys_values)


def query_kernel(qpos_ref, kpos_ref, q_ref, do_ref, stat_ref, k_ref, v_ref, dq_ref):
    @pl.when(pl.program_id(1) == 0)
    def _():
        dq_ref[...] = jnp.zeros_like(dq_ref)

    allowed = kpos_ref[...] <= qpos_ref[...]
    query, d_out, keys, values = q_ref[...], do_ref[...], k_ref[...], v_ref[...]
    parts = []
    for head in range(2):
        lse = stat_ref[0, :, head : head + 1]
        delta = stat_ref[0, :, head + 2 : head + 3]
        scores = jnp.where(allowed, dot_nt(head_only(query, head), keys), masked_score)
        prob = jnp.exp(scores - lse)
        d_prob = dot_nt(head_only(d_out, head), values)
        d_score = (prob * (d_prob - delta)).astype(jnp.bfloat16)
        parts.append(dot_nn(d_score, keys))
    dq_ref[...] += head_pick(parts[0], parts[1]) * HEAD_DIM ** (-0.5)


def query_gradient(query_pos, key_pos, query, d_out, stats, keys_values):
    rows, width = query.shape
    total = keys_values.shape[0]
    chunk = chunk_of(total)
    pairs = width // PAIR
    return pl.pallas_call(
        query_kernel,
        grid=(pairs, total // chunk),
        in_specs=[
            pl.BlockSpec((rows, 1), lambda h, c: (0, 0)),
            pl.BlockSpec((1, chunk), lambda h, c: (0, c)),
            pl.BlockSpec((rows, PAIR), lambda h, c: (0, h)),
            pl.BlockSpec((rows, PAIR), lambda h, c: (0, h)),
            pl.BlockSpec((1, rows, 4), lambda h, c: (h, 0, 0)),
            pl.BlockSpec((chunk, PAIR), lambda h, c: (c, h)),
            pl.BlockSpec((chunk, PAIR), lambda h, c: (c, h + pairs)),
        ],
        out_specs=pl.BlockSpec((rows, PAIR), lambda h, c: (0, h)),
        out_shape=jax.ShapeDtypeStruct((rows, width), jnp.float32),
        compiler_params=pltpu.CompilerParams(vmem_limit_bytes=40 * 2**20),
        cost_estimate=pl.CostEstimate(
            flops=12 * rows * total * width,
            bytes_accessed=4 * total * width,
            transcendentals=rows * total * H,
        ),
        name="attention_query_gradient",
    )(query_pos[:, None], key_pos[None, :], query, d_out, stats, keys_values, keys_values)


def key_kernel(kpos_ref, qpos_ref, k_ref, v_ref, q_ref, do_ref, stat_ref, dk_ref, dv_ref):
    @pl.when(pl.program_id(1) == 0)
    def _():
        dk_ref[...] = jnp.zeros_like(dk_ref)
        dv_ref[...] = jnp.zeros_like(dv_ref)

    allowed = kpos_ref[...] <= qpos_ref[...]
    keys, values, query, d_out = k_ref[...], v_ref[...], q_ref[...], do_ref[...]
    key_parts, value_parts = [], []
    for head in range(2):
        lse = stat_ref[0, head : head + 1, :]
        delta = stat_ref[0, head + 2 : head + 3, :]
        scores = jnp.where(allowed, dot_nt(head_only(keys, head), query), masked_score)
        prob = jnp.exp(scores - lse)
        value_parts.append(dot_nn(prob.astype(jnp.bfloat16), d_out))
        d_prob = dot_nt(head_only(values, head), d_out)
        d_score = (prob * (d_prob - delta)).astype(jnp.bfloat16)
        key_parts.append(dot_nn(d_score, query))
    dk_ref[...] += head_pick(key_parts[0], key_parts[1])
    dv_ref[...] += head_pick(value_parts[0], value_parts[1])


def key_gradients(key_pos, query_pos, qkv, query_all, d_out_all, stats_all):
    rows = qkv.shape[0]
    total, width = query_all.shape
    chunk = chunk_of(total)
    pairs = width // PAIR
    grad_spec = pl.BlockSpec((rows, PAIR), lambda h, c: (0, h))
    return pl.pallas_call(
        key_kernel,
        grid=(pairs, total // chunk),
        in_specs=[
            pl.BlockSpec((rows, 1), lambda h, c: (0, 0)),
            pl.BlockSpec((1, chunk), lambda h, c: (0, c)),
            pl.BlockSpec((rows, PAIR), lambda h, c: (0, h)),
            pl.BlockSpec((rows, PAIR), lambda h, c: (0, h + pairs)),
            pl.BlockSpec((chunk, PAIR), lambda h, c: (c, h)),
            pl.BlockSpec((chunk, PAIR), lambda h, c: (c, h)),
            pl.BlockSpec((1, 4, chunk), lambda h, c: (h, 0, c)),
        ],
        out_specs=[grad_spec, grad_spec],
        out_shape=[jax.ShapeDtypeStruct((rows, width), jnp.float32)] * 2,
        compiler_params=pltpu.CompilerParams(vmem_limit_bytes=40 * 2**20),
        cost_estimate=pl.CostEstimate(
            flops=16 * rows * total * width,
            bytes_accessed=4 * total * width,
            transcendentals=rows * total * H,
        ),
        name="attention_key_gradients",
    )(key_pos[:, None], query_pos[None, :], qkv, qkv, query_all, d_out_all, stats_all)


def whole_weight(weight):
    share = weight.shape[0] // lax.axis_size("ctx")
    mine = lax.dynamic_slice_in_dim(weight, lax.axis_index("ctx") * share, share, 0)
    return lax.all_gather(mine, ("fsdp", "ctx"), axis=0, tiled=True)


def gather_kernel(chips, shards, count, *refs):
    shares, wholes = refs[:count], refs[count : 2 * count]
    own_sem, z_send, z_recv, c_send, c_recv, k_send, k_recv = refs[2 * count :]
    me, row = lax.axis_index("ctx"), lax.axis_index("fsdp")
    chip, core = me // 2, me % 2
    sibling = (chip * 2 + 1 - core, row)

    def above(step):
        return (me, lax.rem(row + step, shards))

    def across(step):
        return (lax.rem(chip + step, chips) * 2 + core, row)

    barrier = pltpu.get_barrier_semaphore()
    greeted = [above(d) for d in range(1, shards)] + [across(d) for d in range(1, chips)]
    greeted.append(sibling)
    for other in greeted:
        pl.semaphore_signal(barrier, inc=1, device_id=other, device_id_type=pl.DeviceIdType.MESH)
    pl.semaphore_wait(barrier, len(greeted))

    def send(src, dst, send_sem, recv_sem, target):
        copy = pltpu.make_async_remote_copy(
            src_ref=src,
            dst_ref=dst,
            send_sem=send_sem,
            recv_sem=recv_sem,
            device_id=target,
            device_id_type=pl.DeviceIdType.MESH,
        )
        copy.start()
        return copy

    def column(item, index):
        return wholes[item].at[:, index]

    own, along, between, inside = {}, {}, {}, {}
    for i in range(count):
        own[i] = pltpu.make_async_copy(shares[i], wholes[i].at[row, me], own_sem.at[i])
        own[i].start()
        for d in range(1, shards):
            along[i, d] = send(
                shares[i],
                wholes[i].at[row, me],
                z_send.at[i, d - 1],
                z_recv.at[i, d - 1],
                above(d),
            )
    for i in range(count):
        own[i].wait()
        for d in range(1, shards):
            along[i, d].wait_recv()
        for d in range(1, chips):
            mine = column(i, me)
            between[i, d] = send(mine, mine, c_send.at[i, d - 1], c_recv.at[i, d - 1], across(d))
        inside[i, 0] = send(
            column(i, me), column(i, me), k_send.at[i, 0], k_recv.at[i, 0], sibling
        )
    for i in range(count):
        for d in range(1, chips):
            between[i, d].wait_recv()
            came = column(i, lax.rem(chip - d + chips, chips) * 2 + core)
            inside[i, d] = send(came, came, k_send.at[i, d], k_recv.at[i, d], sibling)
    for copy in inside.values():
        copy.wait_recv()
    for copies in (along, between, inside):
        for copy in copies.values():
            copy.wait_send()


def whole_weights(weights):
    ctx_count, shards = lax.axis_size("ctx"), lax.axis_size("fsdp")
    chips = ctx_count // 2
    if ctx_count != 8:
        return [whole_weight(item) for item in weights]
    count = len(weights)
    mine = []
    for item in weights:
        share = item.shape[0] // ctx_count
        mine.append(
            lax.dynamic_slice_in_dim(item, lax.axis_index("ctx") * share, share, 0)
        )
    anywhere = pl.BlockSpec(memory_space=pl.ANY)
    dma = pltpu.SemaphoreType.DMA
    wholes = pl.pallas_call(
        partial(gather_kernel, chips, shards, count),
        in_specs=[anywhere] * count,
        out_specs=[anywhere] * count,
        out_shape=[
            jax.ShapeDtypeStruct((shards, ctx_count) + item.shape, item.dtype) for item in mine
        ],
        scratch_shapes=[
            dma((count,)),
            dma((count, shards - 1)),
            dma((count, shards - 1)),
            dma((count, chips - 1)),
            dma((count, chips - 1)),
            dma((count, chips)),
            dma((count, chips)),
        ],
        compiler_params=pltpu.CompilerParams(collective_id=0, has_side_effects=True),
        name="gather_weights",
    )(*mine)
    return [
        whole.reshape(item.shape[0] * shards, item.shape[1])
        for whole, item in zip(wholes, weights)
    ]


def all_positions(pair_table, ctx_count):
    column = jnp.arange(2 * BLK, dtype=jnp.int32)[None, :]
    pair = pair_table[:, None]
    lower = pair * BLK + column
    upper = (2 * ctx_count - 1 - pair) * BLK + column - BLK
    return jnp.where(column < BLK, lower, upper).reshape(-1)


def scatter(term):
    return lax.psum_scatter(term, ("ctx", "fsdp"), scatter_dimension=0, tiled=True)


def per_device(
    layer_in,
    qkv_weight,
    query_bias,
    value_bias,
    out_weight,
    out_bias,
    fc_weight,
    fc_bias,
    proj_weight,
    proj_bias,
    attn_norm_gain,
    attn_norm_shift,
    mlp_norm_gain,
    mlp_norm_shift,
    cotangent,
    pair_table,
):
    ctx_count = lax.axis_size("ctx")
    shards = ctx_count * lax.axis_size("fsdp")
    _, _, rows, width = layer_in.shape
    my_pos = block_positions(pair_table, lax.axis_index("ctx"), ctx_count)
    every_pos = all_positions(pair_table, ctx_count)
    flat_in = layer_in.reshape(rows, width).astype(jnp.float32)
    full_qkv, full_out, full_fc, full_proj = whole_weights(
        (qkv_weight, out_weight, fc_weight, proj_weight)
    )
    normed_one, inverse_one = normalize(flat_in)
    first_in = (normed_one * attn_norm_gain + attn_norm_shift).astype(jnp.bfloat16)
    keys_values = (
        jnp.dot(first_in, full_qkv[:, width:], preferred_element_type=jnp.float32)
        + jnp.concatenate([jnp.zeros_like(value_bias), value_bias])
    ).astype(jnp.bfloat16)
    every_kv = lax.all_gather(keys_values, "ctx", axis=0, tiled=True)
    query = (
        jnp.dot(first_in, full_qkv[:, :width], preferred_element_type=jnp.float32) + query_bias
    ).astype(jnp.bfloat16) * jnp.bfloat16(HEAD_DIM ** (-0.5))
    every_query = lax.all_gather(query, "ctx", axis=0, tiled=True)
    attn_exact, lse = forward_attention(my_pos, every_pos, query, every_kv)
    attended = attn_exact.astype(jnp.bfloat16)
    middle = flat_in + jnp.dot(attended, full_out, preferred_element_type=jnp.float32) + out_bias
    normed_two, inverse_two = normalize(middle)
    second_in = (normed_two * mlp_norm_gain + mlp_norm_shift).astype(jnp.bfloat16)
    pre_act = jnp.dot(second_in, full_fc, preferred_element_type=jnp.float32) + fc_bias
    activated, gelu_back = jax.vjp(partial(jax.nn.gelu, approximate=True), pre_act)
    act_low = activated.astype(jnp.bfloat16)
    result = middle + jnp.dot(act_low, full_proj, preferred_element_type=jnp.float32) + proj_bias
    layer_out = result.astype(jnp.bfloat16).reshape(layer_in.shape)
    d_result = cotangent.reshape(rows, width)
    d_act = jnp.einsum("td,fd->tf", d_result, full_proj, preferred_element_type=jnp.float32)
    (d_pre,) = gelu_back(d_act)
    d_pre_low = d_pre.astype(jnp.bfloat16)
    d_second = jnp.einsum("tf,df->td", d_pre_low, full_fc, preferred_element_type=jnp.float32)
    d_mid_norm, grad_mlp_gain, grad_mlp_shift = norm_back(
        d_second, normed_two, inverse_two, mlp_norm_gain
    )
    d_middle = d_result.astype(jnp.float32) + d_mid_norm
    d_branch = d_middle.astype(jnp.bfloat16)
    d_attended = jnp.einsum(
        "te,de->td", d_branch, full_out, preferred_element_type=jnp.float32
    ).astype(jnp.bfloat16)
    delta = jnp.sum(
        (d_attended.astype(jnp.float32) * attn_exact).reshape(rows, width // PAIR, 2, HEAD_DIM),
        axis=-1,
    )
    stats = jnp.concatenate([lse, jnp.transpose(delta, (1, 0, 2))], axis=-1)
    every_d_out = lax.all_gather(d_attended, "ctx", axis=0, tiled=True)
    every_stat = lax.all_gather(
        jnp.transpose(stats, (0, 2, 1)).reshape(-1, rows), "ctx", axis=1, tiled=True
    ).reshape(width // PAIR, 4, ctx_count * rows)
    grad_proj = jnp.einsum("tf,td->fd", act_low, d_result, preferred_element_type=jnp.float32)
    grad_fc = jnp.einsum("td,tf->df", second_in, d_pre_low, preferred_element_type=jnp.float32)
    grad_out = jnp.einsum("td,te->de", attended, d_branch, preferred_element_type=jnp.float32)
    d_query = query_gradient(my_pos, every_pos, query, d_attended, stats, every_kv)
    d_key, d_value = key_gradients(
        my_pos, every_pos, keys_values, every_query, every_d_out, every_stat
    )
    d_qkv = jnp.concatenate([d_query, d_key, d_value], axis=1).astype(jnp.bfloat16)
    grad_qkv = jnp.einsum("td,te->de", first_in, d_qkv, preferred_element_type=jnp.float32)
    d_first = jnp.einsum("te,de->td", d_qkv, full_qkv, preferred_element_type=jnp.float32)
    d_in_norm, grad_attn_gain, grad_attn_shift = norm_back(
        d_first, normed_one, inverse_one, attn_norm_gain
    )
    grad_in = (d_middle + d_in_norm).reshape(layer_in.shape)
    bias_sum = jnp.sum(d_qkv.astype(jnp.float32), axis=0)
    vectors = (
        bias_sum[:width],
        bias_sum[2 * width :],
        jnp.sum(d_middle, axis=0),
        jnp.sum(d_pre_low.astype(jnp.float32), axis=0),
        jnp.sum(d_result.astype(jnp.float32), axis=0),
        grad_attn_gain,
        grad_attn_shift,
        grad_mlp_gain,
        grad_mlp_shift,
    )
    small = jnp.concatenate([item.reshape(shards, -1) for item in vectors], axis=1)
    lines = 8 * -(-small.shape[1] // (8 * width))
    small = jnp.pad(small, ((0, 0), (0, lines * width - small.shape[1])))
    matrices = (
        [grad_qkv[:, i * width : (i + 1) * width] for i in range(3)]
        + [grad_out]
        + [grad_fc[:, i * width : (i + 1) * width] for i in range(grad_fc.shape[1] // width)]
        + [grad_proj, small.reshape(shards * lines, width)]
    )
    packed = jnp.concatenate(
        [item.astype(jnp.bfloat16).reshape(shards, -1, width) for item in matrices], axis=1
    )
    summed = scatter(packed.reshape(-1, width)).astype(jnp.float32)
    pieces, start = [], 0
    for item in matrices:
        size = item.shape[0] // shards
        pieces.append(summed[start : start + size])
        start += size
    sum_qkv = jnp.concatenate(pieces[:3], axis=1)
    sum_out = pieces[3]
    sum_fc = jnp.concatenate(pieces[4:-2], axis=1)
    sum_proj = pieces[-2]
    sum_small = pieces[-1].reshape(-1)
    small, start = [], 0
    for item in vectors:
        size = item.shape[0] // shards
        small.append(sum_small[start : start + size])
        start += size
    return (
        layer_out,
        grad_in,
        sum_qkv,
        small[0],
        small[1],
        sum_out,
        small[2],
        sum_fc,
        small[3],
        sum_proj,
        small[4],
        small[5],
        small[6],
        small[7],
        small[8],
    )


def solution(mesh):
    return jax.shard_map(
        per_device,
        mesh=mesh,
        in_specs=(
            P("fsdp", "ctx", None, None),
            P("fsdp", None),
            P(),
            P(),
            P("fsdp", None),
            P(),
            P("fsdp", None),
            P(),
            P("fsdp", None),
            P(),
            P(),
            P(),
            P(),
            P(),
            P("fsdp", "ctx", None, None),
            P(),
        ),
        out_specs=(
            P("fsdp", "ctx", None, None),
            P("fsdp", "ctx", None, None),
            P(("ctx", "fsdp"), None),
            P(("ctx", "fsdp")),
            P(("ctx", "fsdp")),
            P(("ctx", "fsdp"), None),
            P(("ctx", "fsdp")),
            P(("ctx", "fsdp"), None),
            P(("ctx", "fsdp")),
            P(("ctx", "fsdp"), None),
            P(("ctx", "fsdp")),
            P(("ctx", "fsdp")),
            P(("ctx", "fsdp")),
            P(("ctx", "fsdp")),
            P(("ctx", "fsdp")),
        ),
        check_vma=False,
    )
```

```python
from functools import partial

import jax
import jax.numpy as jnp
from jax import lax
from jax.experimental import pallas as pl
from jax.experimental.pallas import tpu as pltpu
from jax.sharding import PartitionSpec as P

H = 12
HEAD_DIM = 64
BLK = 96


epsilon = 1e-05
masked_score = -1e30


def normalize(values):
    centered = values - jnp.mean(values, axis=-1, keepdims=True)
    inverse = lax.rsqrt(jnp.mean(centered * centered, axis=-1, keepdims=True) + epsilon)
    return (centered * inverse, inverse)


def norm_back(grad_out, normed, inverse, gain):
    scaled = grad_out * gain
    grad_input = inverse * (
        scaled
        - jnp.mean(scaled, axis=-1, keepdims=True)
        - normed * jnp.mean(scaled * normed, axis=-1, keepdims=True)
    )
    return (grad_input, jnp.sum(grad_out * normed, axis=0), jnp.sum(grad_out, axis=0))


def block_positions(pair_table, device, ctx_count):
    pair_index = lax.dynamic_index_in_dim(pair_table, device, 0, keepdims=False)
    column = jnp.arange(2 * BLK, dtype=jnp.int32)
    lower = pair_index * BLK + column
    upper = (2 * ctx_count - 1 - pair_index) * BLK + column - BLK
    return jnp.where(column < BLK, lower, upper)


PAIR = 2 * HEAD_DIM
CHUNK = 8 * 2 * BLK
NT = (((1,), (1,)), ((), ()))


def chunk_of(total):
    return CHUNK if total % CHUNK == 0 else total


def head_only(block, head):
    lane = lax.broadcasted_iota(jnp.int32, block.shape, 1)
    return jnp.where((lane // HEAD_DIM) == head, block, jnp.zeros_like(block))


def head_pick(first, second):
    lane = lax.broadcasted_iota(jnp.int32, first.shape, 1)
    return jnp.where(lane < HEAD_DIM, first, second)


def dot_nt(left, right):
    return lax.dot_general(left, right, NT, preferred_element_type=jnp.float32)


def dot_nn(left, right):
    return jnp.dot(left, right, preferred_element_type=jnp.float32)


def forward_kernel(qpos_ref, kpos_ref, q_ref, k_ref, v_ref, out_ref, lse_ref, max_ref, sum_ref):
    step = pl.program_id(1)
    last = pl.num_programs(1) - 1

    @pl.when(step == 0)
    def _():
        max_ref[...] = jnp.full_like(max_ref, masked_score)
        sum_ref[...] = jnp.zeros_like(sum_ref)
        out_ref[...] = jnp.zeros_like(out_ref)

    allowed = kpos_ref[...] <= qpos_ref[...]
    query, keys, values = q_ref[...], k_ref[...], v_ref[...]
    mixed, factors = [], []
    for head in range(2):
        scores = jnp.where(allowed, dot_nt(head_only(query, head), keys), masked_score)
        old_max = max_ref[head]
        new_max = jnp.maximum(old_max, jnp.max(scores, axis=-1, keepdims=True))
        expd = jnp.exp(scores - new_max)
        factor = jnp.exp(old_max - new_max)
        sum_ref[head] = sum_ref[head] * factor + jnp.sum(expd, axis=-1, keepdims=True)
        max_ref[head] = new_max
        mixed.append(dot_nn(expd.astype(jnp.bfloat16), values))
        factors.append(factor)
    rows = query.shape[0]
    scale = head_pick(*(jnp.broadcast_to(f, (rows, PAIR)) for f in factors))
    out_ref[...] = out_ref[...] * scale + head_pick(mixed[0], mixed[1])

    @pl.when(step == last)
    def _():
        total = head_pick(*(jnp.broadcast_to(sum_ref[h], (rows, PAIR)) for h in range(2)))
        out_ref[...] = out_ref[...] / total
        lse_ref[0] = jnp.concatenate(
            [max_ref[h] + jnp.log(sum_ref[h]) for h in range(2)], axis=-1
        )


def forward_attention(query_pos, key_pos, query, keys_values):
    rows, width = query.shape
    total = keys_values.shape[0]
    chunk = chunk_of(total)
    pairs = width // PAIR
    return pl.pallas_call(
        forward_kernel,
        grid=(pairs, total // chunk),
        in_specs=[
            pl.BlockSpec((rows, 1), lambda h, c: (0, 0)),
            pl.BlockSpec((1, chunk), lambda h, c: (0, c)),
            pl.BlockSpec((rows, PAIR), lambda h, c: (0, h)),
            pl.BlockSpec((chunk, PAIR), lambda h, c: (c, h)),
            pl.BlockSpec((chunk, PAIR), lambda h, c: (c, h + pairs)),
        ],
        out_specs=[
            pl.BlockSpec((rows, PAIR), lambda h, c: (0, h)),
            pl.BlockSpec((1, rows, 2), lambda h, c: (h, 0, 0)),
        ],
        out_shape=[
            jax.ShapeDtypeStruct((rows, width), jnp.float32),
            jax.ShapeDtypeStruct((pairs, rows, 2), jnp.float32),
        ],
        scratch_shapes=[
            pltpu.VMEM((2, rows, 1), jnp.float32),
            pltpu.VMEM((2, rows, 1), jnp.float32),
        ],
        compiler_params=pltpu.CompilerParams(vmem_limit_bytes=40 * 2**20),
        cost_estimate=pl.CostEstimate(
            flops=8 * rows * total * width,
            bytes_accessed=4 * total * width,
            transcendentals=rows * total * H,
        ),
        name="attention_forward",
    )(query_pos[:, None], key_pos[None, :], query, keys_values, keys_values)


def query_kernel(qpos_ref, kpos_ref, q_ref, do_ref, stat_ref, k_ref, v_ref, dq_ref):
    @pl.when(pl.program_id(1) == 0)
    def _():
        dq_ref[...] = jnp.zeros_like(dq_ref)

    allowed = kpos_ref[...] <= qpos_ref[...]
    query, d_out, keys, values = q_ref[...], do_ref[...], k_ref[...], v_ref[...]
    parts = []
    for head in range(2):
        lse = stat_ref[0, :, head : head + 1]
        delta = stat_ref[0, :, head + 2 : head + 3]
        scores = jnp.where(allowed, dot_nt(head_only(query, head), keys), masked_score)
        prob = jnp.exp(scores - lse)
        d_prob = dot_nt(head_only(d_out, head), values)
        d_score = (prob * (d_prob - delta)).astype(jnp.bfloat16)
        parts.append(dot_nn(d_score, keys))
    dq_ref[...] += head_pick(parts[0], parts[1]) * HEAD_DIM ** (-0.5)


def query_gradient(query_pos, key_pos, query, d_out, stats, keys_values):
    rows, width = query.shape
    total = keys_values.shape[0]
    chunk = chunk_of(total)
    pairs = width // PAIR
    return pl.pallas_call(
        query_kernel,
        grid=(pairs, total // chunk),
        in_specs=[
            pl.BlockSpec((rows, 1), lambda h, c: (0, 0)),
            pl.BlockSpec((1, chunk), lambda h, c: (0, c)),
            pl.BlockSpec((rows, PAIR), lambda h, c: (0, h)),
            pl.BlockSpec((rows, PAIR), lambda h, c: (0, h)),
            pl.BlockSpec((1, rows, 4), lambda h, c: (h, 0, 0)),
            pl.BlockSpec((chunk, PAIR), lambda h, c: (c, h)),
            pl.BlockSpec((chunk, PAIR), lambda h, c: (c, h + pairs)),
        ],
        out_specs=pl.BlockSpec((rows, PAIR), lambda h, c: (0, h)),
        out_shape=jax.ShapeDtypeStruct((rows, width), jnp.float32),
        compiler_params=pltpu.CompilerParams(vmem_limit_bytes=40 * 2**20),
        cost_estimate=pl.CostEstimate(
            flops=12 * rows * total * width,
            bytes_accessed=4 * total * width,
            transcendentals=rows * total * H,
        ),
        name="attention_query_gradient",
    )(query_pos[:, None], key_pos[None, :], query, d_out, stats, keys_values, keys_values)


def key_kernel(kpos_ref, qpos_ref, k_ref, v_ref, q_ref, do_ref, stat_ref, dk_ref, dv_ref):
    @pl.when(pl.program_id(1) == 0)
    def _():
        dk_ref[...] = jnp.zeros_like(dk_ref)
        dv_ref[...] = jnp.zeros_like(dv_ref)

    allowed = kpos_ref[...] <= qpos_ref[...]
    keys, values, query, d_out = k_ref[...], v_ref[...], q_ref[...], do_ref[...]
    key_parts, value_parts = [], []
    for head in range(2):
        lse = stat_ref[0, head : head + 1, :]
        delta = stat_ref[0, head + 2 : head + 3, :]
        scores = jnp.where(allowed, dot_nt(head_only(keys, head), query), masked_score)
        prob = jnp.exp(scores - lse)
        value_parts.append(dot_nn(prob.astype(jnp.bfloat16), d_out))
        d_prob = dot_nt(head_only(values, head), d_out)
        d_score = (prob * (d_prob - delta)).astype(jnp.bfloat16)
        key_parts.append(dot_nn(d_score, query))
    dk_ref[...] += head_pick(key_parts[0], key_parts[1])
    dv_ref[...] += head_pick(value_parts[0], value_parts[1])


def key_gradients(key_pos, query_pos, qkv, query_all, d_out_all, stats_all):
    rows = qkv.shape[0]
    total, width = query_all.shape
    chunk = chunk_of(total)
    pairs = width // PAIR
    grad_spec = pl.BlockSpec((rows, PAIR), lambda h, c: (0, h))
    return pl.pallas_call(
        key_kernel,
        grid=(pairs, total // chunk),
        in_specs=[
            pl.BlockSpec((rows, 1), lambda h, c: (0, 0)),
            pl.BlockSpec((1, chunk), lambda h, c: (0, c)),
            pl.BlockSpec((rows, PAIR), lambda h, c: (0, h)),
            pl.BlockSpec((rows, PAIR), lambda h, c: (0, h + pairs)),
            pl.BlockSpec((chunk, PAIR), lambda h, c: (c, h)),
            pl.BlockSpec((chunk, PAIR), lambda h, c: (c, h)),
            pl.BlockSpec((1, 4, chunk), lambda h, c: (h, 0, c)),
        ],
        out_specs=[grad_spec, grad_spec],
        out_shape=[jax.ShapeDtypeStruct((rows, width), jnp.float32)] * 2,
        compiler_params=pltpu.CompilerParams(vmem_limit_bytes=40 * 2**20),
        cost_estimate=pl.CostEstimate(
            flops=16 * rows * total * width,
            bytes_accessed=4 * total * width,
            transcendentals=rows * total * H,
        ),
        name="attention_key_gradients",
    )(key_pos[:, None], query_pos[None, :], qkv, qkv, query_all, d_out_all, stats_all)


def whole_weight(weight):
    share = weight.shape[0] // lax.axis_size("ctx")
    mine = lax.dynamic_slice_in_dim(weight, lax.axis_index("ctx") * share, share, 0)
    return lax.all_gather(mine, ("fsdp", "ctx"), axis=0, tiled=True)


def gather_kernel(chips, shards, count, *refs):
    shares, wholes = refs[:count], refs[count : 2 * count]
    own_sem, z_send, z_recv, c_send, c_recv, k_send, k_recv = refs[2 * count :]
    me, row = lax.axis_index("ctx"), lax.axis_index("fsdp")
    chip, core = me // 2, me % 2
    sibling = (chip * 2 + 1 - core, row)

    def above(step):
        return (me, lax.rem(row + step, shards))

    def across(step):
        return (lax.rem(chip + step, chips) * 2 + core, row)

    barrier = pltpu.get_barrier_semaphore()
    greeted = [above(d) for d in range(1, shards)] + [across(d) for d in range(1, chips)]
    greeted.append(sibling)
    for other in greeted:
        pl.semaphore_signal(barrier, inc=1, device_id=other, device_id_type=pl.DeviceIdType.MESH)
    pl.semaphore_wait(barrier, len(greeted))

    def send(src, dst, send_sem, recv_sem, target):
        copy = pltpu.make_async_remote_copy(
            src_ref=src,
            dst_ref=dst,
            send_sem=send_sem,
            recv_sem=recv_sem,
            device_id=target,
            device_id_type=pl.DeviceIdType.MESH,
        )
        copy.start()
        return copy

    def column(item, index):
        return wholes[item].at[:, index]

    own, along, between, inside = {}, {}, {}, {}
    for i in range(count):
        own[i] = pltpu.make_async_copy(shares[i], wholes[i].at[row, me], own_sem.at[i])
        own[i].start()
        for d in range(1, shards):
            along[i, d] = send(
                shares[i],
                wholes[i].at[row, me],
                z_send.at[i, d - 1],
                z_recv.at[i, d - 1],
                above(d),
            )
    for i in range(count):
        own[i].wait()
        for d in range(1, shards):
            along[i, d].wait_recv()
        for d in range(1, chips):
            mine = column(i, me)
            between[i, d] = send(mine, mine, c_send.at[i, d - 1], c_recv.at[i, d - 1], across(d))
        inside[i, 0] = send(
            column(i, me), column(i, me), k_send.at[i, 0], k_recv.at[i, 0], sibling
        )
    for i in range(count):
        for d in range(1, chips):
            between[i, d].wait_recv()
            came = column(i, lax.rem(chip - d + chips, chips) * 2 + core)
            inside[i, d] = send(came, came, k_send.at[i, d], k_recv.at[i, d], sibling)
    for copy in inside.values():
        copy.wait_recv()
    for copies in (along, between, inside):
        for copy in copies.values():
            copy.wait_send()


def whole_weights(weights):
    ctx_count, shards = lax.axis_size("ctx"), lax.axis_size("fsdp")
    chips = ctx_count // 2
    if ctx_count != 8:
        return [whole_weight(item) for item in weights]
    count = len(weights)
    mine = []
    for item in weights:
        share = item.shape[0] // ctx_count
        mine.append(
            lax.dynamic_slice_in_dim(item, lax.axis_index("ctx") * share, share, 0)
        )
    anywhere = pl.BlockSpec(memory_space=pl.ANY)
    dma = pltpu.SemaphoreType.DMA
    wholes = pl.pallas_call(
        partial(gather_kernel, chips, shards, count),
        in_specs=[anywhere] * count,
        out_specs=[anywhere] * count,
        out_shape=[
            jax.ShapeDtypeStruct((shards, ctx_count) + item.shape, item.dtype) for item in mine
        ],
        scratch_shapes=[
            dma((count,)),
            dma((count, shards - 1)),
            dma((count, shards - 1)),
            dma((count, chips - 1)),
            dma((count, chips - 1)),
            dma((count, chips)),
            dma((count, chips)),
        ],
        compiler_params=pltpu.CompilerParams(collective_id=0, has_side_effects=True),
        name="gather_weights",
    )(*mine)
    return [
        whole.reshape(item.shape[0] * shards, item.shape[1])
        for whole, item in zip(wholes, weights)
    ]


def scatter_kernel(chips, shards, spans, packed, out, own, k_land, c_land, z_land, *sems):
    local, k_send, k_recv, c_send, c_recv, z_send, z_recv = sems
    me, row = lax.axis_index("ctx"), lax.axis_index("fsdp")
    chip, core = me // 2, me % 2
    sibling = (chip * 2 + 1 - core, row)

    def above(step):
        return (me, lax.rem(row + step, shards))

    def across(step):
        return (lax.rem(chip + step, chips) * 2 + core, row)

    barrier = pltpu.get_barrier_semaphore()
    greeted = [above(d) for d in range(1, shards)] + [across(d) for d in range(1, chips)]
    greeted.append(sibling)
    for other in greeted:
        pl.semaphore_signal(barrier, inc=1, device_id=other, device_id_type=pl.DeviceIdType.MESH)
    pl.semaphore_wait(barrier, len(greeted))

    def send(src, dst, send_sem, recv_sem, target):
        copy = pltpu.make_async_remote_copy(
            src_ref=src,
            dst_ref=dst,
            send_sem=send_sem,
            recv_sem=recv_sem,
            device_id=target,
            device_id_type=pl.DeviceIdType.MESH,
        )
        copy.start()
        return copy

    order = list(range(1, chips)) + [0]
    kept, inside, between, along = {}, {}, {}, {}
    for i, span in enumerate(spans):
        rows = pl.ds(*span)
        for d in order:
            part = lax.rem(chip + d, chips)
            inside[i, d] = send(
                packed.at[part, 1 - core, :, rows],
                k_land.at[part, :, rows],
                k_send.at[i, d],
                k_recv.at[i, d],
                sibling,
            )
            kept[i, d] = pltpu.make_async_copy(
                packed.at[part, core, :, rows], own.at[part, :, rows], local.at[i, d]
            )
            kept[i, d].start()
    for i, span in enumerate(spans):
        rows = pl.ds(*span)
        for d in order:
            part = lax.rem(chip + d, chips)
            kept[i, d].wait()
            inside[i, d].wait_recv()

            @pl.loop(0, shards)
            def _(f):
                total = own[part, f, rows].astype(jnp.float32)
                total += k_land[part, f, rows].astype(jnp.float32)
                own[part, f, rows] = total.astype(jnp.bfloat16)

            if d:
                between[i, d] = send(
                    own.at[part, :, rows],
                    c_land.at[d - 1, :, rows],
                    c_send.at[i, d - 1],
                    c_recv.at[i, d - 1],
                    across(d),
                )
    for i, span in enumerate(spans):
        rows = pl.ds(*span)
        for d in range(1, chips):
            between[i, d].wait_recv()

        @pl.loop(0, shards)
        def _(f):
            total = own[chip, f, rows].astype(jnp.float32)
            for d in range(1, chips):
                total += c_land[d - 1, f, rows].astype(jnp.float32)
            own[chip, f, rows] = total.astype(jnp.bfloat16)

        for d in range(1, shards):
            along[i, d] = send(
                own.at[chip, lax.rem(row + d, shards), rows],
                z_land.at[d - 1, rows],
                z_send.at[i, d - 1],
                z_recv.at[i, d - 1],
                above(d),
            )
    for i, span in enumerate(spans):
        rows = pl.ds(*span)
        for d in range(1, shards):
            along[i, d].wait_recv()
        total = own[chip, row, rows].astype(jnp.float32)
        for d in range(1, shards):
            total += z_land[d - 1, rows].astype(jnp.float32)
        out[rows] = total
    for copies in (inside, between, along):
        for copy in copies.values():
            copy.wait_send()


def scatter_packed(packed):
    ctx_count, shards = lax.axis_size("ctx"), lax.axis_size("fsdp")
    _, rows, width = packed.shape
    if ctx_count != 8:
        return scatter(packed.reshape(-1, width)).astype(jnp.float32)
    chips = ctx_count // 2
    first = 16 * (-(-rows // 32))
    spans = ((0, first), (first, rows - first))
    dma = pltpu.SemaphoreType.DMA
    low = jnp.bfloat16
    return pl.pallas_call(
        partial(scatter_kernel, chips, shards, spans),
        in_specs=[pl.BlockSpec(memory_space=pl.ANY)],
        out_specs=pl.BlockSpec(memory_space=pltpu.VMEM),
        out_shape=jax.ShapeDtypeStruct((rows, width), jnp.float32),
        scratch_shapes=[
            pltpu.VMEM((chips, shards, rows, width), low),
            pltpu.VMEM((chips, shards, rows, width), low),
            pltpu.VMEM((chips - 1, shards, rows, width), low),
            pltpu.VMEM((shards - 1, rows, width), low),
            dma((2, chips)),
            dma((2, chips)),
            dma((2, chips)),
            dma((2, chips - 1)),
            dma((2, chips - 1)),
            dma((2, shards - 1)),
            dma((2, shards - 1)),
        ],
        compiler_params=pltpu.CompilerParams(
            collective_id=1, has_side_effects=True, vmem_limit_bytes=44 * 2**20
        ),
        name="sum_gradients",
    )(packed.reshape(chips, 2, shards, rows, width))


def all_positions(pair_table, ctx_count):
    column = jnp.arange(2 * BLK, dtype=jnp.int32)[None, :]
    pair = pair_table[:, None]
    lower = pair * BLK + column
    upper = (2 * ctx_count - 1 - pair) * BLK + column - BLK
    return jnp.where(column < BLK, lower, upper).reshape(-1)


def scatter(term):
    return lax.psum_scatter(term, ("ctx", "fsdp"), scatter_dimension=0, tiled=True)


def per_device(
    layer_in,
    qkv_weight,
    query_bias,
    value_bias,
    out_weight,
    out_bias,
    fc_weight,
    fc_bias,
    proj_weight,
    proj_bias,
    attn_norm_gain,
    attn_norm_shift,
    mlp_norm_gain,
    mlp_norm_shift,
    cotangent,
    pair_table,
):
    ctx_count = lax.axis_size("ctx")
    shards = ctx_count * lax.axis_size("fsdp")
    _, _, rows, width = layer_in.shape
    my_pos = block_positions(pair_table, lax.axis_index("ctx"), ctx_count)
    every_pos = all_positions(pair_table, ctx_count)
    flat_in = layer_in.reshape(rows, width).astype(jnp.float32)
    full_qkv, full_out, full_fc, full_proj = whole_weights(
        (qkv_weight, out_weight, fc_weight, proj_weight)
    )
    normed_one, inverse_one = normalize(flat_in)
    first_in = (normed_one * attn_norm_gain + attn_norm_shift).astype(jnp.bfloat16)
    keys_values = (
        jnp.dot(first_in, full_qkv[:, width:], preferred_element_type=jnp.float32)
        + jnp.concatenate([jnp.zeros_like(value_bias), value_bias])
    ).astype(jnp.bfloat16)
    every_kv = lax.all_gather(keys_values, "ctx", axis=0, tiled=True)
    query = (
        jnp.dot(first_in, full_qkv[:, :width], preferred_element_type=jnp.float32) + query_bias
    ).astype(jnp.bfloat16) * jnp.bfloat16(HEAD_DIM ** (-0.5))
    every_query = lax.all_gather(query, "ctx", axis=0, tiled=True)
    attn_exact, lse = forward_attention(my_pos, every_pos, query, every_kv)
    attended = attn_exact.astype(jnp.bfloat16)
    middle = flat_in + jnp.dot(attended, full_out, preferred_element_type=jnp.float32) + out_bias
    normed_two, inverse_two = normalize(middle)
    second_in = (normed_two * mlp_norm_gain + mlp_norm_shift).astype(jnp.bfloat16)
    pre_act = jnp.dot(second_in, full_fc, preferred_element_type=jnp.float32) + fc_bias
    activated, gelu_back = jax.vjp(partial(jax.nn.gelu, approximate=True), pre_act)
    act_low = activated.astype(jnp.bfloat16)
    result = middle + jnp.dot(act_low, full_proj, preferred_element_type=jnp.float32) + proj_bias
    layer_out = result.astype(jnp.bfloat16).reshape(layer_in.shape)
    d_result = cotangent.reshape(rows, width)
    d_act = jnp.einsum("td,fd->tf", d_result, full_proj, preferred_element_type=jnp.float32)
    (d_pre,) = gelu_back(d_act)
    d_pre_low = d_pre.astype(jnp.bfloat16)
    d_second = jnp.einsum("tf,df->td", d_pre_low, full_fc, preferred_element_type=jnp.float32)
    d_mid_norm, grad_mlp_gain, grad_mlp_shift = norm_back(
        d_second, normed_two, inverse_two, mlp_norm_gain
    )
    d_middle = d_result.astype(jnp.float32) + d_mid_norm
    d_branch = d_middle.astype(jnp.bfloat16)
    d_attended = jnp.einsum(
        "te,de->td", d_branch, full_out, preferred_element_type=jnp.float32
    ).astype(jnp.bfloat16)
    delta = jnp.sum(
        (d_attended.astype(jnp.float32) * attn_exact).reshape(rows, width // PAIR, 2, HEAD_DIM),
        axis=-1,
    )
    stats = jnp.concatenate([lse, jnp.transpose(delta, (1, 0, 2))], axis=-1)
    every_d_out = lax.all_gather(d_attended, "ctx", axis=0, tiled=True)
    every_stat = lax.all_gather(
        jnp.transpose(stats, (0, 2, 1)).reshape(-1, rows), "ctx", axis=1, tiled=True
    ).reshape(width // PAIR, 4, ctx_count * rows)
    grad_proj = jnp.einsum("tf,td->fd", act_low, d_result, preferred_element_type=jnp.float32)
    grad_fc = jnp.einsum("td,tf->df", second_in, d_pre_low, preferred_element_type=jnp.float32)
    grad_out = jnp.einsum("td,te->de", attended, d_branch, preferred_element_type=jnp.float32)
    d_query = query_gradient(my_pos, every_pos, query, d_attended, stats, every_kv)
    d_key, d_value = key_gradients(
        my_pos, every_pos, keys_values, every_query, every_d_out, every_stat
    )
    d_qkv = jnp.concatenate([d_query, d_key, d_value], axis=1).astype(jnp.bfloat16)
    grad_qkv = jnp.einsum("td,te->de", first_in, d_qkv, preferred_element_type=jnp.float32)
    d_first = jnp.einsum("te,de->td", d_qkv, full_qkv, preferred_element_type=jnp.float32)
    d_in_norm, grad_attn_gain, grad_attn_shift = norm_back(
        d_first, normed_one, inverse_one, attn_norm_gain
    )
    grad_in = (d_middle + d_in_norm).reshape(layer_in.shape)
    bias_sum = jnp.sum(d_qkv.astype(jnp.float32), axis=0)
    vectors = (
        bias_sum[:width],
        bias_sum[2 * width :],
        jnp.sum(d_middle, axis=0),
        jnp.sum(d_pre_low.astype(jnp.float32), axis=0),
        jnp.sum(d_result.astype(jnp.float32), axis=0),
        grad_attn_gain,
        grad_attn_shift,
        grad_mlp_gain,
        grad_mlp_shift,
    )
    small = jnp.concatenate([item.reshape(shards, -1) for item in vectors], axis=1)
    lines = 16 * -(-small.shape[1] // (16 * width))
    small = jnp.pad(small, ((0, 0), (0, lines * width - small.shape[1])))
    matrices = (
        [grad_qkv[:, i * width : (i + 1) * width] for i in range(3)]
        + [grad_out]
        + [grad_fc[:, i * width : (i + 1) * width] for i in range(grad_fc.shape[1] // width)]
        + [grad_proj, small.reshape(shards * lines, width)]
    )
    packed = jnp.concatenate(
        [item.astype(jnp.bfloat16).reshape(shards, -1, width) for item in matrices], axis=1
    )
    summed = scatter_packed(packed)
    pieces, start = [], 0
    for item in matrices:
        size = item.shape[0] // shards
        pieces.append(summed[start : start + size])
        start += size
    sum_qkv = jnp.concatenate(pieces[:3], axis=1)
    sum_out = pieces[3]
    sum_fc = jnp.concatenate(pieces[4:-2], axis=1)
    sum_proj = pieces[-2]
    sum_small = pieces[-1].reshape(-1)
    small, start = [], 0
    for item in vectors:
        size = item.shape[0] // shards
        small.append(sum_small[start : start + size])
        start += size
    return (
        layer_out,
        grad_in,
        sum_qkv,
        small[0],
        small[1],
        sum_out,
        small[2],
        sum_fc,
        small[3],
        sum_proj,
        small[4],
        small[5],
        small[6],
        small[7],
        small[8],
    )


def solution(mesh):
    return jax.shard_map(
        per_device,
        mesh=mesh,
        in_specs=(
            P("fsdp", "ctx", None, None),
            P("fsdp", None),
            P(),
            P(),
            P("fsdp", None),
            P(),
            P("fsdp", None),
            P(),
            P("fsdp", None),
            P(),
            P(),
            P(),
            P(),
            P(),
            P("fsdp", "ctx", None, None),
            P(),
        ),
        out_specs=(
            P("fsdp", "ctx", None, None),
            P("fsdp", "ctx", None, None),
            P(("ctx", "fsdp"), None),
            P(("ctx", "fsdp")),
            P(("ctx", "fsdp")),
            P(("ctx", "fsdp"), None),
            P(("ctx", "fsdp")),
            P(("ctx", "fsdp"), None),
            P(("ctx", "fsdp")),
            P(("ctx", "fsdp"), None),
            P(("ctx", "fsdp")),
            P(("ctx", "fsdp")),
            P(("ctx", "fsdp")),
            P(("ctx", "fsdp")),
            P(("ctx", "fsdp")),
        ),
        check_vma=False,
    )
```
